32 devices in a mesh: tok: 8 (over z, y), mp: 4 (over x, core).
Axes of the slice: x: 2, y: 2, z: 4, core: 2. Of those that a mesh axis runs over, the one named last changes fastest.
Arguments:
- tokens: bfloat16 [8192, 2048], P('tok'), may hold values from -6 to 6
- norm_gain: float32 [2048], replicated, may hold values from 0.1 to 1.9
- w_query: bfloat16 [2048, 2048], P(None, 'mp'), may hold values from -2 to 2
- w_key: bfloat16 [2048, 2048], P(None, 'mp'), may hold values from -2 to 2
- w_value: bfloat16 [2048, 2048], P(None, 'mp'), may hold values from -0.125 to 0.125
- w_out: bfloat16 [2048, 2048], replicated, may hold values from -2.5 to 2.5
- kv_cache: bfloat16 [2, 8192, 2, 2048], P(None, 'tok', None, 'mp'), may hold values from -6 to 6
- wake_blocks: int32 [64, 8], replicated, may hold values from 0 to 63, as said below
- wake_frames: int32 [64, 8], replicated, may hold values from 0 to 1
- wake_counts: int32 [64], replicated, may hold values from 2 to 8, as said below
Outputs:
- advanced: bfloat16 [8192, 2048], P('tok', 'mp')
The draws below stay inside these ranges and needn't reach their ends.
Inputs may be any that keep to these rules, and one draw needn't show every extreme that they name: `wake_blocks`: blocks i * 8 to (i + 1) * 8 - 1 are held by tok index i. Among the live slots (w below the block's count) of the 8 query blocks of one tok index, at most 8 name blocks held by any one tok index, and for every tok index some holder is named exactly 8 times. Slots at or past the count hold any block number. `wake_counts`: some query block has all 8 slots live.
All inputs are finite; a program needn't handle non-finite values.
Results may differ from the reference program's by a relative error of at most 0.005.
The reference program's roundings to bfloat16 on the way (of `normed`, `weights` and `attention`) count: a program that leaves them out, or rounds other values in their place, can miss the bound.
Values may be sent and summed in bfloat16 or wider, within the bound.
A program may use at most 192 MiB of HBM per device.

```python
import math
import jax
import jax.numpy as jnp
from jax import lax

D = 2048
HEADS = 16
HEAD_DIM = 128
BLOCK = 128
WMAX = 8
NF = 2
TOKENS = 8192
QB = 8
NBLK = 64
CAP = 8


def weight_pair(key):
    base_key = jax.random.fold_in(key, 7)
    first_key = jax.random.fold_in(base_key, 1)
    second_key = jax.random.fold_in(base_key, 2)
    spread = 1.0 / math.sqrt(D)
    query_part = jax.random.normal(first_key, (D, D), jnp.float32) * (2.0 * spread)
    key_part = jax.random.normal(second_key, (D, D), jnp.float32) * spread
    return (jnp.clip(query_part, -2.0, 2.0), jnp.clip(key_part, -2.0, 2.0))


def draw_w_query(key, part):
    return weight_pair(key)[0].astype(jnp.bfloat16)


def draw_w_key(key, part):
    return weight_pair(key)[1].astype(jnp.bfloat16)


def permute_one(sub_key):
    return jax.random.permutation(sub_key, NBLK // QB)


def wake_tables(key):
    base_key = jax.random.fold_in(key, 101)
    level_key, jitter_key, top_key, perm_key, pick_key, filler_key = jax.random.split(base_key, 6)
    device_total = NBLK // QB
    slot_total = QB * WMAX
    device_ids = jnp.arange(device_total, dtype=jnp.int32)
    levels = jax.random.randint(level_key, (device_total,), 0, 100)
    topmost = jax.random.randint(top_key, (), 0, device_total)
    levels = jnp.where(device_ids == topmost, 99, levels)
    per_device = 1 + (WMAX - 1) * levels * levels * levels // 970299
    jitter = jax.random.randint(jitter_key, (device_total, QB), -1, 2)
    counts = jnp.clip(per_device[:, None] + jitter, 2, WMAX)
    counts = jnp.where((device_ids == topmost)[:, None], WMAX, counts)
    slot_live = (jnp.arange(WMAX, dtype=jnp.int32)[None, None, :] < counts[:, :, None]).reshape(device_total, slot_total)
    rank_live = jnp.cumsum(slot_live.astype(jnp.int32), axis=1) - 1
    orders = jax.vmap(permute_one)(jax.random.split(perm_key, device_total))
    owners = jnp.take_along_axis(orders, jnp.clip(rank_live // CAP, 0, device_total - 1), axis=1)
    picked = jax.random.randint(pick_key, (device_total, slot_total), 0, QB)
    filler = jax.random.randint(filler_key, (device_total, slot_total), 0, NBLK)
    blocks = jnp.where(slot_live, owners * QB + picked, filler).reshape(NBLK, WMAX)
    return (blocks.astype(jnp.int32), counts.reshape(NBLK).astype(jnp.int32))


def draw_wake_blocks(key, part):
    return wake_tables(key)[0]


def draw_wake_counts(key, part):
    return wake_tables(key)[1]


def touch_ends(entries, own_key, smallest, high):
    spot = [jax.random.randint(jax.random.fold_in(own_key, axis), (), 0, length) for axis, length in enumerate(entries.shape)]
    longest = entries.shape.index(max(entries.shape))
    beside = spot[:longest] + [(spot[longest] + 1) % entries.shape[longest]] + spot[longest + 1:]
    return entries.at[tuple(spot)].set(smallest).at[tuple(beside)].set(high)


def block_levels(stream_key, shape, shards, least, high):
    level, own = 1.0, jax.random.fold_in(stream_key, 6)
    for position, shards_of in shards:
        heights = jnp.exp(jax.random.uniform(jax.random.fold_in(own, position), (shards_of,), jnp.float32, least / len(shards), high / len(shards)))
        level = level * jnp.repeat(heights, shape[position] // shards_of).reshape([-1 if axis == position else 1 for axis in range(len(shape))])
    return level


def bell_draw(key, shape, deviation, reach, cuts=(), kind=jnp.bfloat16):
    values = deviation * jax.random.normal(key, shape, jnp.float32)
    if cuts:
        values = values * block_levels(key, shape, cuts, -0.22, 0.18)
    return jnp.clip(values, -reach, reach).astype(kind)


def setup_inputs(seed: int = 0) -> dict:
    seeds = jax.random.split(jax.random.key(seed), 11)
    return {
        "tokens": bell_draw(seeds[0], (TOKENS, D), 1.0, 6.0, ((0, 8),)),
        "norm_gain": jnp.clip(1.0 + 0.18 * jax.random.normal(seeds[1], (D,), jnp.float32), 0.1, 1.9),
        "w_query": draw_w_query(jax.random.fold_in(seeds[10], 71), 0),
        "w_key": draw_w_key(jax.random.fold_in(seeds[10], 71), 0),
        "w_value": bell_draw(seeds[4], (D, D), D ** -0.5, 0.125, ((1, 4),)),
        "w_out": bell_draw(seeds[5], (D, D), 0.18, 2.5),
        "kv_cache": bell_draw(seeds[6], (NF, TOKENS, 2, D), 1.0, 6.0, ((1, 8), (3, 4))),
        "wake_blocks": draw_wake_blocks(jax.random.fold_in(seeds[10], 71), 0),
        "wake_frames": touch_ends(jax.random.randint(seeds[8], (NBLK, WMAX), 0, NF), jax.random.fold_in(seeds[8], 1), 0, NF - 1).astype(jnp.int32),
        "wake_counts": draw_wake_counts(jax.random.fold_in(seeds[10], 71), 0),
    }


def reference(tokens, norm_gain, w_query, w_key, w_value, w_out, kv_cache, wake_blocks, wake_frames, wake_counts):
    tokens_f32 = tokens.astype(jnp.float32)
    inverse = lax.rsqrt(lax.optimization_barrier(jnp.mean(tokens_f32 * tokens_f32, axis=1, keepdims=True)) + 1e-05)
    normed = (tokens_f32 * inverse * norm_gain[None, :]).astype(jnp.bfloat16)
    queries = jnp.dot(normed, w_query, preferred_element_type=jnp.float32).astype(jnp.bfloat16)
    keys_now = jnp.dot(normed, w_key, preferred_element_type=jnp.float32).astype(jnp.bfloat16)
    values_now = jnp.dot(normed, w_value, preferred_element_type=jnp.float32).astype(jnp.bfloat16)
    query_blocks = queries.reshape(NBLK, BLOCK, HEADS, HEAD_DIM)
    key_blocks = keys_now.reshape(NBLK, BLOCK, HEADS, HEAD_DIM)
    value_blocks = values_now.reshape(NBLK, BLOCK, HEADS, HEAD_DIM)
    cache_keys = kv_cache[:, :, 0, :].reshape(NF, NBLK, BLOCK, HEADS, HEAD_DIM)
    cache_values = kv_cache[:, :, 1, :].reshape(NF, NBLK, BLOCK, HEADS, HEAD_DIM)
    score_scale = 1.0 / math.sqrt(HEAD_DIM)

    def per_block(block_index):
        neighbours = ((block_index + jnp.arange(-1, 2, dtype=jnp.int32)) % NBLK).astype(jnp.int32)
        listed_blocks = wake_blocks[block_index]
        listed_frames = wake_frames[block_index]
        slot_live = jnp.arange(WMAX, dtype=jnp.int32) < wake_counts[block_index]
        key_live = jnp.concatenate([jnp.ones((3 * BLOCK,), bool), jnp.repeat(slot_live, BLOCK)])
        near_keys = key_blocks[neighbours].reshape(3 * BLOCK, HEADS, HEAD_DIM)
        near_values = value_blocks[neighbours].reshape(3 * BLOCK, HEADS, HEAD_DIM)
        far_keys = cache_keys[listed_frames, listed_blocks].reshape(WMAX * BLOCK, HEADS, HEAD_DIM)
        far_values = cache_values[listed_frames, listed_blocks].reshape(WMAX * BLOCK, HEADS, HEAD_DIM)
        every_key = jnp.concatenate([near_keys, far_keys], axis=0).astype(jnp.float32)
        every_value = jnp.concatenate([near_values, far_values], axis=0).astype(jnp.float32)
        scores = jnp.einsum('qhd,khd->hqk', query_blocks[block_index].astype(jnp.float32), every_key) * score_scale
        scores = jnp.where(key_live[None, None, :], scores, -1e+30)
        row_peak = lax.optimization_barrier(jnp.max(scores, axis=2, keepdims=True))
        shifted = jnp.exp(scores - row_peak)
        weights = (shifted / lax.optimization_barrier(jnp.sum(shifted, axis=2, keepdims=True))).astype(jnp.bfloat16)
        result = jnp.einsum('hqk,khd->qhd', weights.astype(jnp.float32), every_value)
        return result.astype(jnp.bfloat16).reshape(BLOCK, D)
    attention = lax.map(per_block, jnp.arange(NBLK, dtype=jnp.int32)).reshape(TOKENS, D)
    projected = jnp.dot(attention, w_out, preferred_element_type=jnp.float32)
    return (tokens_f32 + projected).astype(jnp.bfloat16)
```

```python
import functools
import math

import jax
import jax.numpy as jnp
from jax import lax
from jax.experimental import pallas as pl
from jax.experimental.pallas import tpu as pltpu
from jax.sharding import PartitionSpec as P

HEAD_DIM = 128
BLOCK = 128
WMAX = 8
NEVER = -1e30
SCALE = 1.0 / math.sqrt(HEAD_DIM)
VMEM_BYTES = 40 * 1024 * 1024


def rows_dot(a, b):
    return lax.dot_general(a, b, (((1,), (1,)), ((), ())), preferred_element_type=jnp.float32)


def cols_dot(a, b):
    return lax.dot_general(a, b, (((0,), (0,)), ((), ())), preferred_element_type=jnp.float32)


def head_cols(h):
    return slice(h * HEAD_DIM, (h + 1) * HEAD_DIM)


def near_kernel(heads, q_ref, k0, k1, k2, v0, v1, v2, o_ref, l_ref):
    for h in range(heads):
        cols = head_cols(h)
        q = q_ref[:, cols]
        keys = jnp.concatenate([k0[:, cols], k1[:, cols], k2[:, cols]], axis=0)
        values = jnp.concatenate([v0[:, cols], v1[:, cols], v2[:, cols]], axis=0)
        scores = rows_dot(keys, q) * SCALE
        peak = jnp.max(scores, axis=0, keepdims=True)
        weights = jnp.exp(scores - peak)
        total = jnp.sum(weights, axis=0, keepdims=True)
        out = cols_dot(values, weights.astype(jnp.bfloat16))
        o_ref[0, h] = out / total
        l_ref[0, h : h + 1, :] = peak + jnp.log(total)


def near_attention(queries, keys, values, heads):
    rows, width = queries.shape
    blocks = rows // BLOCK
    spec = [pl.BlockSpec((BLOCK, width), functools.partial(lambda j, b: (b + j, 0), j)) for j in range(3)]
    return pl.pallas_call(
        functools.partial(near_kernel, heads),
        grid=(blocks,),
        in_specs=[pl.BlockSpec((BLOCK, width), lambda b: (b, 0))] + spec + spec,
        out_specs=[
            pl.BlockSpec((1, heads, HEAD_DIM, BLOCK), lambda b: (b, 0, 0, 0)),
            pl.BlockSpec((1, heads, BLOCK), lambda b: (b, 0, 0)),
        ],
        out_shape=[
            jax.ShapeDtypeStruct((blocks, heads, HEAD_DIM, BLOCK), jnp.float32),
            jax.ShapeDtypeStruct((blocks, heads, BLOCK), jnp.float32),
        ],
        compiler_params=pltpu.CompilerParams(vmem_limit_bytes=VMEM_BYTES),
        cost_estimate=pl.CostEstimate(
            flops=4 * rows * 3 * BLOCK * width, bytes_accessed=rows * width * 20, transcendentals=rows * 3 * BLOCK * heads
        ),
    )(queries, keys, keys, keys, values, values, values)


def wake_kernel(heads, idx_ref, cnt_ref, q_ref, table_ref, o_ref, l_ref, acc, peak, total):
    block = pl.program_id(0)
    count = cnt_ref[block]
    width = heads * HEAD_DIM

    @pl.when(count == 0)
    def _():
        o_ref[...] = jnp.zeros_like(o_ref)
        l_ref[...] = jnp.full_like(l_ref, NEVER)

    @pl.when(count > 0)
    def _():
        acc[...] = jnp.zeros_like(acc)
        peak[...] = jnp.full_like(peak, NEVER)
        total[...] = jnp.zeros_like(total)

        def step(s, carry):
            place = idx_ref[block * WMAX + s]
            for h in range(heads):
                cols = head_cols(h)
                keys = table_ref[place, :, cols]
                values = table_ref[place, :, width + h * HEAD_DIM : width + (h + 1) * HEAD_DIM]
                scores = rows_dot(keys, q_ref[0, :, cols]) * SCALE
                old = peak[h : h + 1, :]
                new = jnp.maximum(old, jnp.max(scores, axis=0, keepdims=True))
                weights = jnp.exp(scores - new)
                fade = jnp.exp(old - new)
                peak[h : h + 1, :] = new
                total[h : h + 1, :] = total[h : h + 1, :] * fade + jnp.sum(weights, axis=0, keepdims=True)
                acc[h] = acc[h] * fade + cols_dot(values, weights.astype(jnp.bfloat16))
            return carry

        lax.fori_loop(0, count, step, 0)
        for h in range(heads):
            sums = total[h : h + 1, :]
            o_ref[0, h] = (acc[h] / sums).astype(o_ref.dtype)
            l_ref[0, h : h + 1, :] = peak[h : h + 1, :] + jnp.log(sums)


def wake_attention(every_query, table, places, counts, heads):
    blocks, _, width = every_query.shape
    return pl.pallas_call(
        functools.partial(wake_kernel, heads),
        grid_spec=pltpu.PrefetchScalarGridSpec(
            num_scalar_prefetch=2,
            grid=(blocks,),
            in_specs=[
                pl.BlockSpec((1, BLOCK, width), lambda b, i, c: (b, 0, 0)),
                pl.BlockSpec(table.shape, lambda b, i, c: (0, 0, 0)),
            ],
            out_specs=[
                pl.BlockSpec((1, heads, HEAD_DIM, BLOCK), lambda b, i, c: (b, 0, 0, 0)),
                pl.BlockSpec((1, heads, BLOCK), lambda b, i, c: (b, 0, 0)),
            ],
            scratch_shapes=[
                pltpu.VMEM((heads, HEAD_DIM, BLOCK), jnp.float32),
                pltpu.VMEM((heads, BLOCK), jnp.float32),
                pltpu.VMEM((heads, BLOCK), jnp.float32),
            ],
        ),
        out_shape=[
            jax.ShapeDtypeStruct((blocks, heads, HEAD_DIM, BLOCK), jnp.bfloat16),
            jax.ShapeDtypeStruct((blocks, heads, BLOCK), jnp.float32),
        ],
        compiler_params=pltpu.CompilerParams(vmem_limit_bytes=VMEM_BYTES),
        cost_estimate=pl.CostEstimate(
            flops=blocks * BLOCK * BLOCK * width * 4, bytes_accessed=blocks * BLOCK * width * 4, transcendentals=blocks * BLOCK * BLOCK * heads
        ),
    )(places, counts, every_query, table)


def final_kernel(heads, n_parts, *refs):
    out_ref = refs[-1]
    for h in range(heads):
        logs = [refs[2 * j + 1][0, h : h + 1, :] for j in range(n_parts)]
        peak = functools.reduce(jnp.maximum, logs)
        shares = [jnp.exp(one - peak) for one in logs]
        total = functools.reduce(jnp.add, shares)
        out = jnp.zeros((HEAD_DIM, BLOCK), jnp.float32)
        for j in range(n_parts):
            out += refs[2 * j][0, h].astype(jnp.float32) * (shares[j] / total)
        out_ref[:, head_cols(h)] = out.T.astype(out_ref.dtype)


def final_merge(parts, heads):
    blocks = parts[0][0].shape[0]
    flat, specs = [], []
    for values, logs in parts:
        flat += [values, logs]
        specs += [
            pl.BlockSpec((1, heads, HEAD_DIM, BLOCK), lambda b: (b, 0, 0, 0)),
            pl.BlockSpec((1, heads, BLOCK), lambda b: (b, 0, 0)),
        ]
    return pl.pallas_call(
        functools.partial(final_kernel, heads, len(parts)),
        grid=(blocks,),
        in_specs=specs,
        out_specs=pl.BlockSpec((BLOCK, heads * HEAD_DIM), lambda b: (b, 0)),
        out_shape=jax.ShapeDtypeStruct((blocks * BLOCK, heads * HEAD_DIM), jnp.bfloat16),
        compiler_params=pltpu.CompilerParams(vmem_limit_bytes=VMEM_BYTES),
    )(*flat)


def merge(first, second):
    (o1, l1), (o2, l2) = first, second
    peak = jnp.maximum(l1, l2)
    e1, e2 = jnp.exp(l1 - peak), jnp.exp(l2 - peak)
    total = e1 + e2
    w1, w2 = (e1 / total)[:, :, None, :], (e2 / total)[:, :, None, :]
    out = o1.astype(jnp.float32) * w1 + o2.astype(jnp.float32) * w2
    return out.astype(jnp.bfloat16), peak + jnp.log(total)


def send(part, pairs):
    return tuple(lax.ppermute(leaf, "tok", pairs) for leaf in part)


def live_if(part, flag):
    return part[0], jnp.where(flag, part[1], NEVER)


def return_parts(values, logs, lines):
    place = lax.axis_index("tok")
    z, y = place // 2, place % 2
    across = [(i, i ^ 1) for i in range(2 * lines)]

    def pick(z_to, y_to):
        at = z_to * 2 + y_to
        return tuple(lax.dynamic_index_in_dim(leaf, at, 0, keepdims=False) for leaf in (values, logs))

    ready = {}

    def joined(k):
        k = k % lines
        if k not in ready:
            z_to = (z + k) % lines
            ready[k] = merge(pick(z_to, y), send(pick(z_to, 1 - y), across))
        return ready[k]

    up = down = None
    for k in range(lines - 1, 0, -1):
        here_up, here_down = joined(k), joined(lines - k)
        if up is not None:
            here_up = merge(here_up, live_if(up, z >= 1))
            here_down = merge(here_down, live_if(down, z <= lines - 2))
        up_pairs = [(2 * i + j, 2 * i + 2 + j) for i in range(lines - k) for j in range(2)]
        down_pairs = [(2 * i + j, 2 * i - 2 + j) for i in range(k, lines) for j in range(2)]
        up, down = send(here_up, up_pairs), send(here_down, down_pairs)
    own = joined(0)
    return [own, live_if(up, z >= 1), live_if(down, z <= lines - 2)]


def on_device(
    tokens,
    norm_gain,
    w_query,
    w_key,
    w_value,
    w_out,
    kv_cache,
    wake_blocks,
    wake_frames,
    wake_counts,
):
    tok_rows = tokens.shape[0]
    local_width = w_query.shape[1]
    heads = local_width // HEAD_DIM
    blocks_dev = tok_rows // BLOCK
    tok_devices = lax.axis_size("tok")
    tok_place = lax.axis_index("tok")
    model_place = lax.axis_index("mp")
    tokens_f32 = tokens.astype(jnp.float32)
    inverse = lax.rsqrt(jnp.mean(tokens_f32 * tokens_f32, axis=1, keepdims=True) + 1e-05)
    normed = (tokens_f32 * inverse * norm_gain[None, :]).astype(jnp.bfloat16)
    queries = jnp.dot(normed, w_query, preferred_element_type=jnp.float32).astype(jnp.bfloat16)
    every_query = lax.all_gather(queries, "tok", axis=0, tiled=True)
    keys_now = jnp.dot(normed, w_key, preferred_element_type=jnp.float32).astype(jnp.bfloat16)
    values_now = jnp.dot(normed, w_value, preferred_element_type=jnp.float32).astype(jnp.bfloat16)
    forward = [(i, (i + 1) % tok_devices) for i in range(tok_devices)]
    backward = [(j, i) for i, j in forward]

    def with_halo(rows):
        low = lax.ppermute(rows[tok_rows - BLOCK :], "tok", forward)
        high = lax.ppermute(rows[:BLOCK], "tok", backward)
        return jnp.concatenate([low, rows, high], axis=0)

    near = near_attention(queries, with_halo(keys_now), with_halo(values_now), heads)

    live = jnp.arange(WMAX, dtype=jnp.int32)[None, :] < wake_counts[:, None]
    held = live & (wake_blocks // blocks_dev == tok_place)
    position = jnp.cumsum(held.astype(jnp.int32), axis=1) - 1
    local_index = wake_frames * blocks_dev + wake_blocks % blocks_dev
    picked = held[:, None, :] & (position[:, None, :] == jnp.arange(WMAX, dtype=jnp.int32)[None, :, None])
    places = jnp.sum(jnp.where(picked, local_index[:, None, :], 0), axis=2).reshape(-1)
    counts = jnp.sum(held.astype(jnp.int32), axis=1)
    table = kv_cache.reshape(kv_cache.shape[0] * blocks_dev, BLOCK, 2 * local_width)
    far_values, far_logs = wake_attention(
        every_query.reshape(-1, BLOCK, local_width), table, places, counts, heads
    )
    shape = (tok_devices, blocks_dev, heads)
    parts = return_parts(
        far_values.reshape(shape + (HEAD_DIM, BLOCK)), far_logs.reshape(shape + (BLOCK,)), tok_devices // 2
    )
    attention = final_merge([tuple(near)] + parts, heads)
    gathered = lax.all_gather(attention, "mp", axis=1, tiled=True)
    out_cols = lax.dynamic_slice_in_dim(w_out, model_place * local_width, local_width, 1)
    mixed = jnp.dot(gathered, out_cols, preferred_element_type=jnp.float32)
    residual_part = lax.dynamic_slice_in_dim(tokens, model_place * local_width, local_width, 1)
    return (residual_part.astype(jnp.float32) + mixed).astype(jnp.bfloat16)


def solution(mesh):
    return jax.shard_map(
        on_device,
        mesh=mesh,
        in_specs=(
            P("tok", None),
            P(),
            P(None, "mp"),
            P(None, "mp"),
            P(None, "mp"),
            P(),
            P(None, "tok", None, "mp"),
            P(),
            P(),
            P(),
        ),
        out_specs=P("tok", "mp"),
        check_vma=False,
    )
```

```python
import functools
import math

import jax
import jax.numpy as jnp
from jax import lax
from jax.experimental import pallas as pl
from jax.experimental.pallas import tpu as pltpu
from jax.sharding import PartitionSpec as P

HEAD_DIM = 128
BLOCK = 128
WMAX = 8
NEVER = -1e30
SCALE = 1.0 / math.sqrt(HEAD_DIM)
VMEM_BYTES = 40 * 1024 * 1024


def rows_dot(a, b):
    return lax.dot_general(a, b, (((1,), (1,)), ((), ())), preferred_element_type=jnp.float32)


def cols_dot(a, b):
    return lax.dot_general(a, b, (((0,), (0,)), ((), ())), preferred_element_type=jnp.float32)


def head_cols(h):
    return slice(h * HEAD_DIM, (h + 1) * HEAD_DIM)


def near_kernel(heads, q_ref, k0, k1, k2, v0, v1, v2, o_ref, l_ref):
    for h in range(heads):
        cols = head_cols(h)
        q = q_ref[:, cols]
        keys = jnp.concatenate([k0[:, cols], k1[:, cols], k2[:, cols]], axis=0)
        values = jnp.concatenate([v0[:, cols], v1[:, cols], v2[:, cols]], axis=0)
        scores = rows_dot(keys, q) * SCALE
        peak = jnp.max(scores, axis=0, keepdims=True)
        weights = jnp.exp(scores - peak)
        total = jnp.sum(weights, axis=0, keepdims=True)
        out = cols_dot(values, weights.astype(jnp.bfloat16))
        o_ref[0, h] = out / total
        l_ref[0, h : h + 1, :] = peak + jnp.log(total)


def near_attention(queries, keys, values, heads):
    rows, width = queries.shape
    blocks = rows // BLOCK
    spec = [pl.BlockSpec((BLOCK, width), functools.partial(lambda j, b: (b + j, 0), j)) for j in range(3)]
    return pl.pallas_call(
        functools.partial(near_kernel, heads),
        grid=(blocks,),
        in_specs=[pl.BlockSpec((BLOCK, width), lambda b: (b, 0))] + spec + spec,
        out_specs=[
            pl.BlockSpec((1, heads, HEAD_DIM, BLOCK), lambda b: (b, 0, 0, 0)),
            pl.BlockSpec((1, heads, BLOCK), lambda b: (b, 0, 0)),
        ],
        out_shape=[
            jax.ShapeDtypeStruct((blocks, heads, HEAD_DIM, BLOCK), jnp.float32),
            jax.ShapeDtypeStruct((blocks, heads, BLOCK), jnp.float32),
        ],
        compiler_params=pltpu.CompilerParams(vmem_limit_bytes=VMEM_BYTES),
        cost_estimate=pl.CostEstimate(
            flops=4 * rows * 3 * BLOCK * width, bytes_accessed=rows * width * 20, transcendentals=rows * 3 * BLOCK * heads
        ),
    )(queries, keys, keys, keys, values, values, values)


def wake_kernel(heads, idx_ref, cnt_ref, q_ref, table_ref, o_ref, l_ref, acc, peak, total):
    block = pl.program_id(0)
    count = cnt_ref[block]
    width = heads * HEAD_DIM

    @pl.when(count == 0)
    def _():
        o_ref[...] = jnp.zeros_like(o_ref)
        l_ref[...] = jnp.full_like(l_ref, NEVER)

    @pl.when(count > 0)
    def _():
        acc[...] = jnp.zeros_like(acc)
        peak[...] = jnp.full_like(peak, NEVER)
        total[...] = jnp.zeros_like(total)

        def step(s, carry):
            place = idx_ref[block * WMAX + s]
            for h in range(heads):
                cols = head_cols(h)
                keys = table_ref[place, :, cols]
                values = table_ref[place, :, width + h * HEAD_DIM : width + (h + 1) * HEAD_DIM]
                scores = rows_dot(keys, q_ref[0, :, cols]) * SCALE
                old = peak[h : h + 1, :]
                new = jnp.maximum(old, jnp.max(scores, axis=0, keepdims=True))
                weights = jnp.exp(scores - new)
                fade = jnp.exp(old - new)
                peak[h : h + 1, :] = new
                total[h : h + 1, :] = total[h : h + 1, :] * fade + jnp.sum(weights, axis=0, keepdims=True)
                acc[h] = acc[h] * fade + cols_dot(values, weights.astype(jnp.bfloat16))
            return carry

        lax.fori_loop(0, count, step, 0)
        for h in range(heads):
            sums = total[h : h + 1, :]
            o_ref[0, h] = (acc[h] / sums).astype(o_ref.dtype)
            l_ref[0, h : h + 1, :] = peak[h : h + 1, :] + jnp.log(sums)


def wake_attention(some_query, table, places, counts, heads):
    blocks, _, width = some_query.shape
    return pl.pallas_call(
        functools.partial(wake_kernel, heads),
        grid_spec=pltpu.PrefetchScalarGridSpec(
            num_scalar_prefetch=2,
            grid=(blocks,),
            in_specs=[
                pl.BlockSpec((1, BLOCK, width), lambda b, i, c: (b, 0, 0)),
                pl.BlockSpec(table.shape, lambda b, i, c: (0, 0, 0)),
            ],
            out_specs=[
                pl.BlockSpec((1, heads, HEAD_DIM, BLOCK), lambda b, i, c: (b, 0, 0, 0)),
                pl.BlockSpec((1, heads, BLOCK), lambda b, i, c: (b, 0, 0)),
            ],
            scratch_shapes=[
                pltpu.VMEM((heads, HEAD_DIM, BLOCK), jnp.float32),
                pltpu.VMEM((heads, BLOCK), jnp.float32),
                pltpu.VMEM((heads, BLOCK), jnp.float32),
            ],
        ),
        out_shape=[
            jax.ShapeDtypeStruct((blocks, heads, HEAD_DIM, BLOCK), jnp.bfloat16),
            jax.ShapeDtypeStruct((blocks, heads, BLOCK), jnp.float32),
        ],
        compiler_params=pltpu.CompilerParams(vmem_limit_bytes=VMEM_BYTES),
        cost_estimate=pl.CostEstimate(
            flops=blocks * BLOCK * BLOCK * width * 4, bytes_accessed=blocks * BLOCK * width * 32, transcendentals=blocks * BLOCK * BLOCK * heads
        ),
    )(places, counts, some_query, table)


def final_kernel(heads, n_parts, *refs):
    out_ref = refs[-1]
    for h in range(heads):
        logs = [refs[2 * j + 1][0, h : h + 1, :] for j in range(n_parts)]
        peak = functools.reduce(jnp.maximum, logs)
        shares = [jnp.exp(one - peak) for one in logs]
        total = functools.reduce(jnp.add, shares)
        out = jnp.zeros((HEAD_DIM, BLOCK), jnp.float32)
        for j in range(n_parts):
            out += refs[2 * j][0, h].astype(jnp.float32) * (shares[j] / total)
        out_ref[:, head_cols(h)] = out.T.astype(out_ref.dtype)


def final_merge(parts, heads):
    blocks = parts[0][0].shape[0]
    flat, specs = [], []
    for values, logs in parts:
        flat += [values, logs]
        specs += [
            pl.BlockSpec((1, heads, HEAD_DIM, BLOCK), lambda b: (b, 0, 0, 0)),
            pl.BlockSpec((1, heads, BLOCK), lambda b: (b, 0, 0)),
        ]
    return pl.pallas_call(
        functools.partial(final_kernel, heads, len(parts)),
        grid=(blocks,),
        in_specs=specs,
        out_specs=pl.BlockSpec((BLOCK, heads * HEAD_DIM), lambda b: (b, 0)),
        out_shape=jax.ShapeDtypeStruct((blocks * BLOCK, heads * HEAD_DIM), jnp.bfloat16),
        compiler_params=pltpu.CompilerParams(vmem_limit_bytes=VMEM_BYTES),
    )(*flat)


def merge(first, second):
    (o1, l1), (o2, l2) = first, second
    peak = jnp.maximum(l1, l2)
    e1, e2 = jnp.exp(l1 - peak), jnp.exp(l2 - peak)
    total = e1 + e2
    w1, w2 = (e1 / total)[:, :, None, :], (e2 / total)[:, :, None, :]
    out = o1.astype(jnp.float32) * w1 + o2.astype(jnp.float32) * w2
    return out.astype(jnp.bfloat16), peak + jnp.log(total)


def send(part, pairs):
    return tuple(lax.ppermute(leaf, "tok", pairs) for leaf in part)


def live_if(part, flag):
    return part[0], jnp.where(flag, part[1], NEVER)


def up_pairs(lines, hops):
    return [(2 * i + j, 2 * i + 2 + j) for i in range(hops - 1, lines - 1) for j in range(2)]


def down_pairs(lines, hops):
    return [(2 * i + j, 2 * i - 2 + j) for i in range(1, lines + 1 - hops) for j in range(2)]


def arrivals(lines):
    table = []
    for z in range(lines):
        order = sorted((i for i in range(lines) if i != z), key=lambda i: (abs(i - z), (i + z) % 2 == 0, i))
        table.append([z] + order)
    return table


def gather_queries(queries, lines):
    place = lax.axis_index("tok")
    z = place // 2
    across = [(i, i ^ 1) for i in range(2 * lines)]
    ups, downs = [queries], [queries]
    others = [lax.ppermute(queries, "tok", across)]
    for hops in range(1, lines):
        ups.append(lax.ppermute(ups[-1], "tok", up_pairs(lines, hops)))
        downs.append(lax.ppermute(downs[-1], "tok", down_pairs(lines, hops)))
    mine = [queries]
    table = arrivals(lines)
    pieces = {}
    for hops in range(1, lines):
        pieces[hops], pieces[-hops] = ups[hops], downs[hops]
    for j in range(1, lines):
        chosen, used = None, []
        for row in range(lines):
            hops = row - table[row][j]
            piece = pieces[hops]
            used.append(hops)
            chosen = piece if chosen is None else jnp.where(z == row, piece, chosen)
        used = sorted(set(used))
        chosen, *after = lax.optimization_barrier([chosen] + [pieces[hops] for hops in used])
        pieces.update(zip(used, after))
        mine.append(chosen)
        others.append(lax.ppermute(chosen, "tok", across))
    return mine, others


def return_parts(get_part, lines):
    place = lax.axis_index("tok")
    z, y = place // 2, place % 2
    across = [(i, i ^ 1) for i in range(2 * lines)]
    table = arrivals(lines)
    slots = []
    for j in range(lines):
        z_to = lookup([table[row][j] for row in range(lines)], z)
        away = send(get_part(j, z_to * 2 + 1 - y, True), across)
        slots.append(merge(get_part(j, z_to * 2 + y, False), away))

    def joined(shift):
        chosen = None
        for row in range(lines):
            piece = slots[table[row].index((row + shift) % lines)]
            if chosen is None:
                chosen = piece
            else:
                chosen = tuple(jnp.where(z == row, p, c) for p, c in zip(piece, chosen))
        return chosen

    up = down = None
    for k in range(lines - 1, 0, -1):
        here_up, here_down = joined(k), joined(-k)
        if up is not None:
            here_up = merge(here_up, live_if(up, z >= 1))
            here_down = merge(here_down, live_if(down, z <= lines - 2))
        go_up = [(2 * i + j, 2 * i + 2 + j) for i in range(lines - k) for j in range(2)]
        go_down = [(2 * i + j, 2 * i - 2 + j) for i in range(k, lines) for j in range(2)]
        up, down = send(here_up, go_up), send(here_down, go_down)
    return [slots[0], live_if(up, z >= 1), live_if(down, z <= lines - 2)]


def lookup(values, at):
    out = jnp.int32(values[0])
    for i, value in enumerate(values):
        out = jnp.where(at == i, jnp.int32(value), out)
    return out


def project_out(attention, out_cols):
    width = attention.shape[1]
    count = lax.axis_size("mp")
    if count != 4:
        gathered = lax.all_gather(attention, "mp", axis=1, tiled=True)
        return jnp.dot(gathered, out_cols, preferred_element_type=jnp.float32)
    place = lax.axis_index("mp")

    def swap(piece, bit):
        return lax.ppermute(piece, "mp", [(i, i ^ bit) for i in range(count)])

    def product(piece, source):
        rows = lax.dynamic_slice_in_dim(out_cols, source * width, width, 0)
        return jnp.dot(piece, rows, preferred_element_type=jnp.float32)

    far, near = swap(attention, 2), swap(attention, 1)
    last = swap(far, 1)
    total = product(attention, place) + product(near, place ^ 1)
    return total + product(far, place ^ 2) + product(last, place ^ 3)


def on_device(
    tokens,
    norm_gain,
    w_query,
    w_key,
    w_value,
    w_out,
    kv_cache,
    wake_blocks,
    wake_frames,
    wake_counts,
):
    tok_rows = tokens.shape[0]
    local_width = w_query.shape[1]
    heads = local_width // HEAD_DIM
    blocks_dev = tok_rows // BLOCK
    tok_devices = lax.axis_size("tok")
    tok_place = lax.axis_index("tok")
    model_place = lax.axis_index("mp")
    tokens_f32 = tokens.astype(jnp.float32)
    inverse = lax.rsqrt(jnp.mean(tokens_f32 * tokens_f32, axis=1, keepdims=True) + 1e-05)
    normed = (tokens_f32 * inverse * norm_gain[None, :]).astype(jnp.bfloat16)
    queries = jnp.dot(normed, w_query, preferred_element_type=jnp.float32).astype(jnp.bfloat16)
    mine, others = gather_queries(queries, tok_devices // 2)
    keys_now = jnp.dot(normed, w_key, preferred_element_type=jnp.float32).astype(jnp.bfloat16)
    values_now = jnp.dot(normed, w_value, preferred_element_type=jnp.float32).astype(jnp.bfloat16)
    forward = [(i, (i + 1) % tok_devices) for i in range(tok_devices)]
    backward = [(j, i) for i, j in forward]

    def with_halo(rows):
        low = lax.ppermute(rows[tok_rows - BLOCK :], "tok", forward)
        high = lax.ppermute(rows[:BLOCK], "tok", backward)
        return jnp.concatenate([low, rows, high], axis=0)

    near = near_attention(queries, with_halo(keys_now), with_halo(values_now), heads)

    live = jnp.arange(WMAX, dtype=jnp.int32)[None, :] < wake_counts[:, None]
    held = live & (wake_blocks // blocks_dev == tok_place)
    position = jnp.cumsum(held.astype(jnp.int32), axis=1) - 1
    local_index = wake_frames * blocks_dev + wake_blocks % blocks_dev
    picked = held[:, None, :] & (position[:, None, :] == jnp.arange(WMAX, dtype=jnp.int32)[None, :, None])
    places = jnp.sum(jnp.where(picked, local_index[:, None, :], 0), axis=2).reshape(-1)
    counts = jnp.sum(held.astype(jnp.int32), axis=1)
    table = kv_cache.reshape(kv_cache.shape[0] * blocks_dev, BLOCK, 2 * local_width)
    places, counts = places.reshape(tok_devices, -1), counts.reshape(tok_devices, -1)

    def get_part(slot, reader, other):
        piece = (others if other else mine)[slot].reshape(blocks_dev, BLOCK, local_width)
        return wake_attention(
            piece,
            table,
            lax.dynamic_index_in_dim(places, reader, 0, keepdims=False),
            lax.dynamic_index_in_dim(counts, reader, 0, keepdims=False),
            heads,
        )

    parts = return_parts(get_part, tok_devices // 2)
    attention = final_merge([tuple(near)] + parts, heads)
    out_cols = lax.dynamic_slice_in_dim(w_out, model_place * local_width, local_width, 1)
    mixed = project_out(attention, out_cols)
    residual_part = lax.dynamic_slice_in_dim(tokens, model_place * local_width, local_width, 1)
    return (residual_part.astype(jnp.float32) + mixed).astype(jnp.bfloat16)


def solution(mesh):
    return jax.shard_map(
        on_device,
        mesh=mesh,
        in_specs=(
            P("tok", None),
            P(),
            P(None, "mp"),
            P(None, "mp"),
            P(None, "mp"),
            P(),
            P(None, "tok", None, "mp"),
            P(),
            P(),
            P(),
        ),
        out_specs=P("tok", "mp"),
        check_vma=False,
    )
```

```python
import functools
import math

import jax
import jax.numpy as jnp
from jax import lax
from jax.experimental import pallas as pl
from jax.experimental.pallas import tpu as pltpu
from jax.sharding import PartitionSpec as P

HEAD_DIM = 128
BLOCK = 128
WMAX = 8
NEVER = -1e30
SCALE = 1.0 / math.sqrt(HEAD_DIM)
VMEM_BYTES = 40 * 1024 * 1024


def rows_dot(a, b):
    return lax.dot_general(a, b, (((1,), (1,)), ((), ())), preferred_element_type=jnp.float32)


def cols_dot(a, b):
    return lax.dot_general(a, b, (((0,), (0,)), ((), ())), preferred_element_type=jnp.float32)


def head_cols(h):
    return slice(h * HEAD_DIM, (h + 1) * HEAD_DIM)


def near_kernel(heads, q_ref, k0, k1, k2, v0, v1, v2, o_ref, l_ref):
    for h in range(heads):
        cols = head_cols(h)
        q = q_ref[:, cols]
        keys = jnp.concatenate([k0[:, cols], k1[:, cols], k2[:, cols]], axis=0)
        values = jnp.concatenate([v0[:, cols], v1[:, cols], v2[:, cols]], axis=0)
        scores = rows_dot(keys, q) * SCALE
        peak = jnp.max(scores, axis=0, keepdims=True)
        weights = jnp.exp(scores - peak)
        total = jnp.sum(weights, axis=0, keepdims=True)
        out = cols_dot(values, weights.astype(jnp.bfloat16))
        o_ref[0, h] = out / total
        l_ref[0, h : h + 1, :] = peak + jnp.log(total)


def near_attention(queries, keys, values, heads):
    rows, width = queries.shape
    blocks = rows // BLOCK
    spec = [pl.BlockSpec((BLOCK, width), functools.partial(lambda j, b: (b + j, 0), j)) for j in range(3)]
    return pl.pallas_call(
        functools.partial(near_kernel, heads),
        grid=(blocks,),
        in_specs=[pl.BlockSpec((BLOCK, width), lambda b: (b, 0))] + spec + spec,
        out_specs=[
            pl.BlockSpec((1, heads, HEAD_DIM, BLOCK), lambda b: (b, 0, 0, 0)),
            pl.BlockSpec((1, heads, BLOCK), lambda b: (b, 0, 0)),
        ],
        out_shape=[
            jax.ShapeDtypeStruct((blocks, heads, HEAD_DIM, BLOCK), jnp.float32),
            jax.ShapeDtypeStruct((blocks, heads, BLOCK), jnp.float32),
        ],
        compiler_params=pltpu.CompilerParams(vmem_limit_bytes=VMEM_BYTES),
        cost_estimate=pl.CostEstimate(
            flops=4 * rows * 3 * BLOCK * width, bytes_accessed=rows * width * 20, transcendentals=rows * 3 * BLOCK * heads
        ),
    )(queries, keys, keys, keys, values, values, values)


def wake_kernel(heads, idx_ref, cnt_ref, q_ref, table_ref, o_ref, l_ref, acc, peak, total):
    block = pl.program_id(0)
    count = cnt_ref[block]
    width = heads * HEAD_DIM

    @pl.when(count == 0)
    def _():
        o_ref[...] = jnp.zeros_like(o_ref)
        l_ref[...] = jnp.full_like(l_ref, NEVER)

    @pl.when(count > 0)
    def _():
        acc[...] = jnp.zeros_like(acc)
        peak[...] = jnp.full_like(peak, NEVER)
        total[...] = jnp.zeros_like(total)

        def step(s, carry):
            place = idx_ref[block * WMAX + s]
            for h in range(heads):
                cols = head_cols(h)
                keys = table_ref[place, :, cols]
                values = table_ref[place, :, width + h * HEAD_DIM : width + (h + 1) * HEAD_DIM]
                scores = rows_dot(keys, q_ref[0, :, cols]) * SCALE
                old = peak[h : h + 1, :]
                new = jnp.maximum(old, jnp.max(scores, axis=0, keepdims=True))
                weights = jnp.exp(scores - new)
                fade = jnp.exp(old - new)
                peak[h : h + 1, :] = new
                total[h : h + 1, :] = total[h : h + 1, :] * fade + jnp.sum(weights, axis=0, keepdims=True)
                acc[h] = acc[h] * fade + cols_dot(values, weights.astype(jnp.bfloat16))
            return carry

        lax.fori_loop(0, count, step, 0)
        for h in range(heads):
            sums = total[h : h + 1, :]
            o_ref[0, h] = (acc[h] / sums).astype(o_ref.dtype)
            l_ref[0, h : h + 1, :] = peak[h : h + 1, :] + jnp.log(sums)


def wake_attention(some_query, table, places, counts, heads):
    blocks, _, width = some_query.shape
    return pl.pallas_call(
        functools.partial(wake_kernel, heads),
        grid_spec=pltpu.PrefetchScalarGridSpec(
            num_scalar_prefetch=2,
            grid=(blocks,),
            in_specs=[
                pl.BlockSpec((1, BLOCK, width), lambda b, i, c: (b, 0, 0)),
                pl.BlockSpec(table.shape, lambda b, i, c: (0, 0, 0)),
            ],
            out_specs=[
                pl.BlockSpec((1, heads, HEAD_DIM, BLOCK), lambda b, i, c: (b, 0, 0, 0)),
                pl.BlockSpec((1, heads, BLOCK), lambda b, i, c: (b, 0, 0)),
            ],
            scratch_shapes=[
                pltpu.VMEM((heads, HEAD_DIM, BLOCK), jnp.float32),
                pltpu.VMEM((heads, BLOCK), jnp.float32),
                pltpu.VMEM((heads, BLOCK), jnp.float32),
            ],
        ),
        out_shape=[
            jax.ShapeDtypeStruct((blocks, heads, HEAD_DIM, BLOCK), jnp.bfloat16),
            jax.ShapeDtypeStruct((blocks, heads, BLOCK), jnp.float32),
        ],
        compiler_params=pltpu.CompilerParams(vmem_limit_bytes=VMEM_BYTES),
        cost_estimate=pl.CostEstimate(
            flops=blocks * BLOCK * BLOCK * width * 4, bytes_accessed=blocks * BLOCK * width * 32, transcendentals=blocks * BLOCK * BLOCK * heads
        ),
    )(places, counts, some_query, table)


def final_kernel(heads, n_parts, *refs):
    out_ref = refs[-1]
    for h in range(heads):
        logs = [refs[2 * j + 1][0, h : h + 1, :] for j in range(n_parts)]
        peak = functools.reduce(jnp.maximum, logs)
        shares = [jnp.exp(one - peak) for one in logs]
        total = functools.reduce(jnp.add, shares)
        out = jnp.zeros((HEAD_DIM, BLOCK), jnp.float32)
        for j in range(n_parts):
            out += refs[2 * j][0, h].astype(jnp.float32) * (shares[j] / total)
        out_ref[:, head_cols(h)] = out.T.astype(out_ref.dtype)


def final_merge(parts, heads):
    blocks = parts[0][0].shape[0]
    flat, specs = [], []
    for values, logs in parts:
        flat += [values, logs]
        specs += [
            pl.BlockSpec((1, heads, HEAD_DIM, BLOCK), lambda b: (b, 0, 0, 0)),
            pl.BlockSpec((1, heads, BLOCK), lambda b: (b, 0, 0)),
        ]
    return pl.pallas_call(
        functools.partial(final_kernel, heads, len(parts)),
        grid=(blocks,),
        in_specs=specs,
        out_specs=pl.BlockSpec((BLOCK, heads * HEAD_DIM), lambda b: (b, 0)),
        out_shape=jax.ShapeDtypeStruct((blocks * BLOCK, heads * HEAD_DIM), jnp.bfloat16),
        compiler_params=pltpu.CompilerParams(vmem_limit_bytes=VMEM_BYTES),
    )(*flat)


def merge(first, second):
    (o1, l1), (o2, l2) = first, second
    peak = jnp.maximum(l1, l2)
    e1, e2 = jnp.exp(l1 - peak), jnp.exp(l2 - peak)
    total = e1 + e2
    w1, w2 = (e1 / total)[:, :, None, :], (e2 / total)[:, :, None, :]
    out = o1.astype(jnp.float32) * w1 + o2.astype(jnp.float32) * w2
    return out.astype(jnp.bfloat16), peak + jnp.log(total)


def send(part, pairs):
    return tuple(lax.ppermute(leaf, "tok", pairs) for leaf in part)


def live_if(part, flag):
    return part[0], jnp.where(flag, part[1], NEVER)


def up_pairs(lines, hops):
    return [(2 * i + j, 2 * i + 2 + j) for i in range(hops - 1, lines - 1) for j in range(2)]


def down_pairs(lines, hops):
    return [(2 * i + j, 2 * i - 2 + j) for i in range(1, lines + 1 - hops) for j in range(2)]


def arrivals(lines):
    table = []
    for z in range(lines):
        order = sorted((i for i in range(lines) if i != z), key=lambda i: (abs(i - z), (i + z) % 2 == 0, i))
        table.append([z] + order)
    return table


def hold(*things):
    return lax.optimization_barrier(things)


def out_and_back(queries, lines, first_work, second_work, wake):
    place = lax.axis_index("tok")
    z, y = place // 2, place % 2
    across = [(i, i ^ 1) for i in range(2 * lines)]
    table = arrivals(lines)

    def z_of(slot):
        return lookup([table[row][slot] for row in range(lines)], z)

    def wake_pair(slot, mine, other, side):
        near_part = wake(mine, z_of(slot) * 2 + y, side)
        far_part = wake(other, z_of(slot) * 2 + 1 - y, side)
        return near_part, far_part

    pieces = {0: queries}
    mine, others, parts, side = [queries], [], [], None
    for step in range(lines):
        other = lax.ppermute(mine[step], "tok", across)
        going = {}
        if step < lines - 1:
            going[step + 1] = lax.ppermute(pieces[step], "tok", up_pairs(lines, step + 1))
            going[-step - 1] = lax.ppermute(pieces[-step], "tok", down_pairs(lines, step + 1))
        work = ()
        if step == 0:
            work = first_work()
        else:
            if step == 1:
                near = second_work(side)
                work += (near,)
            work += (wake_pair(step - 1, mine[step - 1], others[step - 1], side),)
        other, going, work = hold(other, going, work)
        others.append(other)
        pieces.update(going)
        if step == 0:
            side = work
        else:
            if step == 1:
                near = work[0]
            parts.append(work[-1])
        if step < lines - 1:
            chosen = None
            for row in range(lines):
                piece = pieces[row - table[row][step + 1]]
                chosen = piece if chosen is None else jnp.where(z == row, piece, chosen)
            mine.append(chosen)

    slots = {}
    last = lines - 1
    away = send(wake(others[last], z_of(last) * 2 + 1 - y, side), across)
    kept = wake(mine[last], z_of(last) * 2 + y, side)
    away, kept = hold(away, kept)
    slots[last] = merge(kept, away)

    def joined(shift):
        chosen = None
        for row in range(lines):
            if not 0 <= row + shift < lines:
                continue
            piece = slots[table[row].index(row + shift)]
            if chosen is None:
                chosen = piece
            else:
                chosen = tuple(jnp.where(z == row, p, c) for p, c in zip(piece, chosen))
        return chosen

    up = down = None
    for k in range(last, 0, -1):
        here_up, here_down = joined(k), joined(-k)
        if up is not None:
            here_up = merge(here_up, live_if(up, z >= 1))
            here_down = merge(here_down, live_if(down, z <= last - 1))
        go_up = [(2 * i + j, 2 * i + 2 + j) for i in range(lines - k) for j in range(2)]
        go_down = [(2 * i + j, 2 * i - 2 + j) for i in range(k, lines) for j in range(2)]
        kept, leaving = parts[k - 1]
        leaving, here_up, here_down = hold(leaving, here_up, here_down)
        up, down, away = hold(send(here_up, go_up), send(here_down, go_down), send(leaving, across))
        slots[k - 1] = merge(kept, away) if k > 1 else None
    return near, [kept, away, live_if(up, z >= 1), live_if(down, z <= last - 1)]


def lookup(values, at):
    out = jnp.int32(values[0])
    for i, value in enumerate(values):
        out = jnp.where(at == i, jnp.int32(value), out)
    return out


def project_out(attention, out_cols):
    width = attention.shape[1]
    count = lax.axis_size("mp")
    if count != 4:
        gathered = lax.all_gather(attention, "mp", axis=1, tiled=True)
        return jnp.dot(gathered, out_cols, preferred_element_type=jnp.float32)
    place = lax.axis_index("mp")

    def swap(piece, bit):
        return lax.ppermute(piece, "mp", [(i, i ^ bit) for i in range(count)])

    def product(piece, source):
        rows = lax.dynamic_slice_in_dim(out_cols, source * width, width, 0)
        return jnp.dot(piece, rows, preferred_element_type=jnp.float32)

    far, near = swap(attention, 2), swap(attention, 1)
    far, near, total = hold(far, near, product(attention, place))
    last = swap(far, 1)
    total += product(near, place ^ 1) + product(far, place ^ 2)
    last, total = hold(last, total)
    return total + product(last, place ^ 3)


def on_device(
    tokens,
    norm_gain,
    w_query,
    w_key,
    w_value,
    w_out,
    kv_cache,
    wake_blocks,
    wake_frames,
    wake_counts,
):
    tok_rows = tokens.shape[0]
    local_width = w_query.shape[1]
    heads = local_width // HEAD_DIM
    blocks_dev = tok_rows // BLOCK
    tok_devices = lax.axis_size("tok")
    tok_place = lax.axis_index("tok")
    model_place = lax.axis_index("mp")
    tokens_f32 = tokens.astype(jnp.float32)
    inverse = lax.rsqrt(jnp.mean(tokens_f32 * tokens_f32, axis=1, keepdims=True) + 1e-05)
    normed = (tokens_f32 * inverse * norm_gain[None, :]).astype(jnp.bfloat16)
    queries = jnp.dot(normed, w_query, preferred_element_type=jnp.float32).astype(jnp.bfloat16)
    forward = [(i, (i + 1) % tok_devices) for i in range(tok_devices)]
    backward = [(j, i) for i, j in forward]

    def with_halo(rows):
        low = lax.ppermute(rows[tok_rows - BLOCK :], "tok", forward)
        high = lax.ppermute(rows[:BLOCK], "tok", backward)
        return jnp.concatenate([low, rows, high], axis=0)

    live = jnp.arange(WMAX, dtype=jnp.int32)[None, :] < wake_counts[:, None]
    held = live & (wake_blocks // blocks_dev == tok_place)
    position = jnp.cumsum(held.astype(jnp.int32), axis=1) - 1
    local_index = wake_frames * blocks_dev + wake_blocks % blocks_dev
    picked = held[:, None, :] & (position[:, None, :] == jnp.arange(WMAX, dtype=jnp.int32)[None, :, None])
    places = jnp.sum(jnp.where(picked, local_index[:, None, :], 0), axis=2).reshape(-1)
    counts = jnp.sum(held.astype(jnp.int32), axis=1)
    places, counts = places.reshape(tok_devices, -1), counts.reshape(tok_devices, -1)

    def first_work():
        keys_now = jnp.dot(normed, w_key, preferred_element_type=jnp.float32).astype(jnp.bfloat16)
        values_now = jnp.dot(normed, w_value, preferred_element_type=jnp.float32).astype(jnp.bfloat16)
        table = kv_cache.reshape(kv_cache.shape[0] * blocks_dev, BLOCK, 2 * local_width)
        return with_halo(keys_now), with_halo(values_now), table

    def second_work(side):
        return tuple(near_attention(queries, side[0], side[1], heads))

    def wake(piece, reader, side):
        return tuple(
            wake_attention(
                piece.reshape(blocks_dev, BLOCK, local_width),
                side[2],
                lax.dynamic_index_in_dim(places, reader, 0, keepdims=False),
                lax.dynamic_index_in_dim(counts, reader, 0, keepdims=False),
                heads,
            )
        )

    near, parts = out_and_back(queries, tok_devices // 2, first_work, second_work, wake)
    attention = final_merge([near] + parts, heads)
    out_cols = lax.dynamic_slice_in_dim(w_out, model_place * local_width, local_width, 1)
    mixed = project_out(attention, out_cols)
    residual_part = lax.dynamic_slice_in_dim(tokens, model_place * local_width, local_width, 1)
    return (residual_part.astype(jnp.float32) + mixed).astype(jnp.bfloat16)


def solution(mesh):
    return jax.shard_map(
        on_device,
        mesh=mesh,
        in_specs=(
            P("tok", None),
            P(),
            P(None, "mp"),
            P(None, "mp"),
            P(None, "mp"),
            P(),
            P(None, "tok", None, "mp"),
            P(),
            P(),
            P(),
        ),
        out_specs=P("tok", "mp"),
        check_vma=False,
    )
```

```python
import functools
import math

import jax
import jax.numpy as jnp
from jax import lax
from jax.experimental import pallas as pl
from jax.experimental.pallas import tpu as pltpu
from jax.sharding import PartitionSpec as P

HEAD_DIM = 128
BLOCK = 128
WMAX = 8
NEVER = -1e30
SCALE = 1.0 / math.sqrt(HEAD_DIM)
VMEM_BYTES = 40 * 1024 * 1024


def rows_dot(a, b):
    return lax.dot_general(a, b, (((1,), (1,)), ((), ())), preferred_element_type=jnp.float32)


def cols_dot(a, b):
    return lax.dot_general(a, b, (((0,), (0,)), ((), ())), preferred_element_type=jnp.float32)


def head_cols(h):
    return slice(h * HEAD_DIM, (h + 1) * HEAD_DIM)


def near_kernel(heads, q_ref, k0, k1, k2, v0, v1, v2, o_ref, l_ref):
    for h in range(heads):
        cols = head_cols(h)
        q = q_ref[:, cols]
        keys = jnp.concatenate([k0[:, cols], k1[:, cols], k2[:, cols]], axis=0)
        values = jnp.concatenate([v0[:, cols], v1[:, cols], v2[:, cols]], axis=0)
        scores = rows_dot(keys, q) * SCALE
        peak = jnp.max(scores, axis=0, keepdims=True)
        weights = jnp.exp(scores - peak)
        total = jnp.sum(weights, axis=0, keepdims=True)
        out = cols_dot(values, weights.astype(jnp.bfloat16))
        o_ref[0, h] = out / total
        l_ref[0, h : h + 1, :] = peak + jnp.log(total)


def near_attention(queries, keys, values, heads):
    rows, width = queries.shape
    blocks = rows // BLOCK
    spec = [pl.BlockSpec((BLOCK, width), functools.partial(lambda j, b: (b + j, 0), j)) for j in range(3)]
    return pl.pallas_call(
        functools.partial(near_kernel, heads),
        grid=(blocks,),
        in_specs=[pl.BlockSpec((BLOCK, width), lambda b: (b, 0))] + spec + spec,
        out_specs=[
            pl.BlockSpec((1, heads, HEAD_DIM, BLOCK), lambda b: (b, 0, 0, 0)),
            pl.BlockSpec((1, heads, BLOCK), lambda b: (b, 0, 0)),
        ],
        out_shape=[
            jax.ShapeDtypeStruct((blocks, heads, HEAD_DIM, BLOCK), jnp.float32),
            jax.ShapeDtypeStruct((blocks, heads, BLOCK), jnp.float32),
        ],
        compiler_params=pltpu.CompilerParams(vmem_limit_bytes=VMEM_BYTES),
        cost_estimate=pl.CostEstimate(
            flops=4 * rows * 3 * BLOCK * width, bytes_accessed=rows * width * 20, transcendentals=rows * 3 * BLOCK * heads
        ),
    )(queries, keys, keys, keys, values, values, values)


def wake_kernel(heads, idx_ref, cnt_ref, q_ref, table_ref, o_ref, l_ref, acc, peak, total):
    block = pl.program_id(0)
    count = cnt_ref[block]
    width = heads * HEAD_DIM

    @pl.when(count == 0)
    def _():
        o_ref[...] = jnp.zeros_like(o_ref)
        l_ref[...] = jnp.full_like(l_ref, NEVER)

    @pl.when(count > 0)
    def _():
        acc[...] = jnp.zeros_like(acc)
        peak[...] = jnp.full_like(peak, NEVER)
        total[...] = jnp.zeros_like(total)

        def step(s, carry):
            place = idx_ref[block * WMAX + s]
            for h in range(heads):
                cols = head_cols(h)
                keys = table_ref[place, :, cols]
                values = table_ref[place, :, width + h * HEAD_DIM : width + (h + 1) * HEAD_DIM]
                scores = rows_dot(keys, q_ref[0, :, cols]) * SCALE
                old = peak[h : h + 1, :]
                new = jnp.maximum(old, jnp.max(scores, axis=0, keepdims=True))
                weights = jnp.exp(scores - new)
                fade = jnp.exp(old - new)
                peak[h : h + 1, :] = new
                total[h : h + 1, :] = total[h : h + 1, :] * fade + jnp.sum(weights, axis=0, keepdims=True)
                acc[h] = acc[h] * fade + cols_dot(values, weights.astype(jnp.bfloat16))
            return carry

        lax.fori_loop(0, count, step, 0)
        for h in range(heads):
            sums = total[h : h + 1, :]
            o_ref[0, h] = (acc[h] / sums).astype(o_ref.dtype)
            l_ref[0, h : h + 1, :] = peak[h : h + 1, :] + jnp.log(sums)


def wake_attention(some_query, table, places, counts, heads):
    blocks, _, width = some_query.shape
    return pl.pallas_call(
        functools.partial(wake_kernel, heads),
        grid_spec=pltpu.PrefetchScalarGridSpec(
            num_scalar_prefetch=2,
            grid=(blocks,),
            in_specs=[
                pl.BlockSpec((1, BLOCK, width), lambda b, i, c: (b, 0, 0)),
                pl.BlockSpec(table.shape, lambda b, i, c: (0, 0, 0)),
            ],
            out_specs=[
                pl.BlockSpec((1, heads, HEAD_DIM, BLOCK), lambda b, i, c: (b, 0, 0, 0)),
                pl.BlockSpec((1, heads, BLOCK), lambda b, i, c: (b, 0, 0)),
            ],
            scratch_shapes=[
                pltpu.VMEM((heads, HEAD_DIM, BLOCK), jnp.float32),
                pltpu.VMEM((heads, BLOCK), jnp.float32),
                pltpu.VMEM((heads, BLOCK), jnp.float32),
            ],
        ),
        out_shape=[
            jax.ShapeDtypeStruct((blocks, heads, HEAD_DIM, BLOCK), jnp.bfloat16),
            jax.ShapeDtypeStruct((blocks, heads, BLOCK), jnp.float32),
        ],
        compiler_params=pltpu.CompilerParams(vmem_limit_bytes=VMEM_BYTES),
        cost_estimate=pl.CostEstimate(
            flops=blocks * BLOCK * BLOCK * width * 4, bytes_accessed=blocks * BLOCK * width * 32, transcendentals=blocks * BLOCK * BLOCK * heads
        ),
    )(places, counts, some_query, table)


def final_kernel(heads, n_parts, *refs):
    out_ref = refs[-1]
    for h in range(heads):
        logs = [refs[2 * j + 1][0, h : h + 1, :] for j in range(n_parts)]
        peak = functools.reduce(jnp.maximum, logs)
        shares = [jnp.exp(one - peak) for one in logs]
        total = functools.reduce(jnp.add, shares)
        out = jnp.zeros((HEAD_DIM, BLOCK), jnp.float32)
        for j in range(n_parts):
            out += refs[2 * j][0, h].astype(jnp.float32) * (shares[j] / total)
        out_ref[:, head_cols(h)] = out.T.astype(out_ref.dtype)


def final_merge(parts, heads):
    blocks = parts[0][0].shape[0]
    flat, specs = [], []
    for values, logs in parts:
        flat += [values, logs]
        specs += [
            pl.BlockSpec((1, heads, HEAD_DIM, BLOCK), lambda b: (b, 0, 0, 0)),
            pl.BlockSpec((1, heads, BLOCK), lambda b: (b, 0, 0)),
        ]
    return pl.pallas_call(
        functools.partial(final_kernel, heads, len(parts)),
        grid=(blocks,),
        in_specs=specs,
        out_specs=pl.BlockSpec((BLOCK, heads * HEAD_DIM), lambda b: (b, 0)),
        out_shape=jax.ShapeDtypeStruct((blocks * BLOCK, heads * HEAD_DIM), jnp.bfloat16),
        compiler_params=pltpu.CompilerParams(vmem_limit_bytes=VMEM_BYTES),
    )(*flat)


def merge(first, second):
    (o1, l1), (o2, l2) = first, second
    peak = jnp.maximum(l1, l2)
    e1, e2 = jnp.exp(l1 - peak), jnp.exp(l2 - peak)
    total = e1 + e2
    w1, w2 = (e1 / total)[:, :, None, :], (e2 / total)[:, :, None, :]
    out = o1.astype(jnp.float32) * w1 + o2.astype(jnp.float32) * w2
    return out.astype(jnp.bfloat16), peak + jnp.log(total)


def send(part, pairs):
    return tuple(lax.ppermute(leaf, "tok", pairs) for leaf in part)


def live_if(part, flag):
    return part[0], jnp.where(flag, part[1], NEVER)


def up_pairs(lines, hops):
    return [(2 * i + j, 2 * i + 2 + j) for i in range(hops - 1, lines - 1) for j in range(2)]


def down_pairs(lines, hops):
    return [(2 * i + j, 2 * i - 2 + j) for i in range(1, lines + 1 - hops) for j in range(2)]


def arrivals(lines):
    table = []
    for z in range(lines):
        order = sorted((i for i in range(lines) if i != z), key=lambda i: (abs(i - z), (i + z) % 2 == 0, i))
        table.append([z] + order)
    return table


def hold(*things):
    return lax.optimization_barrier(things)


def out_and_back(queries, lines, project, add_halo, attend_near, wake):
    place = lax.axis_index("tok")
    z, y = place // 2, place % 2
    across = [(i, i ^ 1) for i in range(2 * lines)]
    table = arrivals(lines)

    def z_of(slot):
        return lookup([table[row][slot] for row in range(lines)], z)

    def wake_pair(slot, mine, other, side):
        near_part = wake(mine, z_of(slot) * 2 + y, side)
        far_part = wake(other, z_of(slot) * 2 + 1 - y, side)
        return near_part, far_part

    pieces = {0: queries}
    mine, others, parts, side = [queries], [], {}, None
    for step in range(lines):
        other = lax.ppermute(mine[step], "tok", across)
        going = {}
        if step < lines - 1:
            going[step + 1] = lax.ppermute(pieces[step], "tok", up_pairs(lines, step + 1))
            going[-step - 1] = lax.ppermute(pieces[-step], "tok", down_pairs(lines, step + 1))
        work = {}
        if step == 0:
            work["side"] = project()
        elif step != 2:
            work["part"] = wake_pair(step - 1, mine[step - 1], others[step - 1], side)
        if step == lines - 1:
            work["halo"] = add_halo(side)
        other, going, work = hold(other, going, work)
        others.append(other)
        pieces.update(going)
        side = work.get("side", side)
        if "part" in work:
            parts[step - 1] = work["part"]
        halo = work.get("halo")
        if step < lines - 1:
            chosen = None
            for row in range(lines):
                piece = pieces[row - table[row][step + 1]]
                chosen = piece if chosen is None else jnp.where(z == row, piece, chosen)
            mine.append(chosen)

    slots = {}
    last = lines - 1
    away = send(wake(others[last], z_of(last) * 2 + 1 - y, side), across)
    kept = wake(mine[last], z_of(last) * 2 + y, side)
    away, kept = hold(away, kept)
    slots[last] = merge(kept, away)

    def joined(shift):
        chosen = None
        for row in range(lines):
            if not 0 <= row + shift < lines:
                continue
            piece = slots[table[row].index(row + shift)]
            if chosen is None:
                chosen = piece
            else:
                chosen = tuple(jnp.where(z == row, p, c) for p, c in zip(piece, chosen))
        return chosen

    up = down = None
    for k in range(last, 0, -1):
        here_up, here_down = joined(k), joined(-k)
        if up is not None:
            here_up = merge(here_up, live_if(up, z >= 1))
            here_down = merge(here_down, live_if(down, z <= last - 1))
        go_up = [(2 * i + j, 2 * i + 2 + j) for i in range(lines - k) for j in range(2)]
        go_down = [(2 * i + j, 2 * i - 2 + j) for i in range(k, lines) for j in range(2)]
        kept, leaving = parts[k - 1]
        leaving, here_up, here_down = hold(leaving, here_up, here_down)
        work = {}
        if k == last:
            work["part"] = wake_pair(1, mine[1], others[1], side)
        if k == last - 1:
            work["near"] = attend_near(halo)
        up, down, away, work = hold(send(here_up, go_up), send(here_down, go_down), send(leaving, across), work)
        if k == last:
            parts[1] = work["part"]
        near = work.get("near", None if k >= last - 1 else near)
        slots[k - 1] = merge(kept, away) if k > 1 else None
    return near, [kept, away, live_if(up, z >= 1), live_if(down, z <= last - 1)]


def lookup(values, at):
    out = jnp.int32(values[0])
    for i, value in enumerate(values):
        out = jnp.where(at == i, jnp.int32(value), out)
    return out


def project_out(attention, out_cols):
    width = attention.shape[1]
    count = lax.axis_size("mp")
    if count != 4:
        gathered = lax.all_gather(attention, "mp", axis=1, tiled=True)
        return jnp.dot(gathered, out_cols, preferred_element_type=jnp.float32)
    place = lax.axis_index("mp")

    def swap(piece, bit):
        return lax.ppermute(piece, "mp", [(i, i ^ bit) for i in range(count)])

    def product(piece, source):
        rows = lax.dynamic_slice_in_dim(out_cols, source * width, width, 0)
        return jnp.dot(piece, rows, preferred_element_type=jnp.float32)

    far, near = swap(attention, 2), swap(attention, 1)
    far, near, total = hold(far, near, product(attention, place))
    last = swap(far, 1)
    total += product(near, place ^ 1) + product(far, place ^ 2)
    last, total = hold(last, total)
    return total + product(last, place ^ 3)


def on_device(
    tokens,
    norm_gain,
    w_query,
    w_key,
    w_value,
    w_out,
    kv_cache,
    wake_blocks,
    wake_frames,
    wake_counts,
):
    tok_rows = tokens.shape[0]
    local_width = w_query.shape[1]
    heads = local_width // HEAD_DIM
    blocks_dev = tok_rows // BLOCK
    tok_devices = lax.axis_size("tok")
    tok_place = lax.axis_index("tok")
    model_place = lax.axis_index("mp")
    tokens_f32 = tokens.astype(jnp.float32)
    inverse = lax.rsqrt(jnp.mean(tokens_f32 * tokens_f32, axis=1, keepdims=True) + 1e-05)
    normed = (tokens_f32 * inverse * norm_gain[None, :]).astype(jnp.bfloat16)
    queries = jnp.dot(normed, w_query, preferred_element_type=jnp.float32).astype(jnp.bfloat16)
    forward = [(i, (i + 1) % tok_devices) for i in range(tok_devices)]
    backward = [(j, i) for i, j in forward]

    def with_halo(rows):
        low = lax.ppermute(rows[tok_rows - BLOCK :], "tok", forward)
        high = lax.ppermute(rows[:BLOCK], "tok", backward)
        return jnp.concatenate([low, rows, high], axis=0)

    live = jnp.arange(WMAX, dtype=jnp.int32)[None, :] < wake_counts[:, None]
    held = live & (wake_blocks // blocks_dev == tok_place)
    position = jnp.cumsum(held.astype(jnp.int32), axis=1) - 1
    local_index = wake_frames * blocks_dev + wake_blocks % blocks_dev
    picked = held[:, None, :] & (position[:, None, :] == jnp.arange(WMAX, dtype=jnp.int32)[None, :, None])
    places = jnp.sum(jnp.where(picked, local_index[:, None, :], 0), axis=2).reshape(-1)
    counts = jnp.sum(held.astype(jnp.int32), axis=1)
    places, counts = places.reshape(tok_devices, -1), counts.reshape(tok_devices, -1)

    def project():
        keys_now = jnp.dot(normed, w_key, preferred_element_type=jnp.float32).astype(jnp.bfloat16)
        values_now = jnp.dot(normed, w_value, preferred_element_type=jnp.float32).astype(jnp.bfloat16)
        table = kv_cache.reshape(kv_cache.shape[0] * blocks_dev, BLOCK, 2 * local_width)
        return keys_now, values_now, table

    def add_halo(side):
        return with_halo(side[0]), with_halo(side[1])

    def attend_near(halo):
        return tuple(near_attention(queries, halo[0], halo[1], heads))

    def wake(piece, reader, side):
        return tuple(
            wake_attention(
                piece.reshape(blocks_dev, BLOCK, local_width),
                side[2],
                lax.dynamic_index_in_dim(places, reader, 0, keepdims=False),
                lax.dynamic_index_in_dim(counts, reader, 0, keepdims=False),
                heads,
            )
        )

    near, parts = out_and_back(queries, tok_devices // 2, project, add_halo, attend_near, wake)
    attention = final_merge([near] + parts, heads)
    out_cols = lax.dynamic_slice_in_dim(w_out, model_place * local_width, local_width, 1)
    mixed = project_out(attention, out_cols)
    residual_part = lax.dynamic_slice_in_dim(tokens, model_place * local_width, local_width, 1)
    return (residual_part.astype(jnp.float32) + mixed).astype(jnp.bfloat16)


def solution(mesh):
    return jax.shard_map(
        on_device,
        mesh=mesh,
        in_specs=(
            P("tok", None),
            P(),
            P(None, "mp"),
            P(None, "mp"),
            P(None, "mp"),
            P(),
            P(None, "tok", None, "mp"),
            P(),
            P(),
            P(),
        ),
        out_specs=P("tok", "mp"),
        check_vma=False,
    )
```
